128 devices in a mesh: grp: 16 (over x, y), hist: 8 (over z, core).
Axes of the slice: x: 4, y: 4, z: 4, core: 2. Of those that a mesh axis runs over, the one named last changes fastest.
Arguments:
- cand_tokens: bfloat16 [32768, 1024], P(('grp', 'hist')), may hold values from -6 to 6
- cand_user: int32 [32768], P('grp'), may hold values from 0 to 1
- hist_len: int32 [32], P('grp'), may hold values from 1 to 8192
- req_owner: int32 [16, 8, 16, 1], P('grp', 'hist'), may hold values from 0 to 15; in each aligned block of 16 rows (0 to 15, 16 to 31, ..., all dimensions but the last counted through in order) at most 2 rows name the same one
- req_slot: int32 [16, 8, 16], P('grp', 'hist'), may hold values from 0 to 15
- hist_embed: bfloat16 [256, 8, 128, 1024], P('grp', 'hist'), may hold values from -6 to 6
- w_query: bfloat16 [1024, 1024], replicated, may hold values from -0.1875 to 0.1875
- w_key: bfloat16 [1024, 1024], replicated, may hold values from -0.1875 to 0.1875
- w_value: bfloat16 [1024, 1024], replicated, may hold values from -0.1875 to 0.1875
- w_gate: bfloat16 [1024, 1024], replicated, may hold values from -0.1875 to 0.1875
- w_out: bfloat16 [1024, 1024], replicated, may hold values from -0.1875 to 0.1875
Outputs:
- ranked: bfloat16 [32768, 1024], P(('grp', 'hist'))
The draws below stay inside these ranges and needn't reach their ends.
Inputs may be any that keep to these rules, and one draw needn't show every extreme that they name: `req_owner`: at most 2 of one device's 16 requests name the same owner, and in every draw some device sends exactly 2 to one owner.
All inputs are finite; a program needn't handle non-finite values.
Results may differ from the reference program's by a relative error of at most 0.0053.
Values may be sent and summed in bfloat16 or wider, within the bound.
A program may use at most 128 MiB of HBM per device.

```python
import math
import jax
import jax.numpy as jnp
import numpy as np
from jax import lax

D = 1024
HEADS = 8
HD = 128
BLK = 128
BPS = 8
USR_GRP = 2
CAND_GRP = 2048
CANDS = 32768
USERS = 32
HLEN = 8192
REQ = 16
OWN_DEV = 16
CAP = 2
N_GRP = 16
N_HIST = 8


def touch_ends(drawn, key, low, top_value):
    spot = [jax.random.randint(jax.random.fold_in(key, axis), (), 0, length) for axis, length in enumerate(drawn.shape)]
    main_axis = drawn.shape.index(max(drawn.shape))
    beside = spot[:main_axis] + [(spot[main_axis] + 1) % drawn.shape[main_axis]] + spot[main_axis + 1:]
    return drawn.at[tuple(spot)].set(low).at[tuple(beside)].set(top_value)


def block_levels(stream_key, dims, cuts, smallest, top_value):
    level, own = 1.0, jax.random.fold_in(stream_key, 6)
    for dim, shards_of in cuts:
        steps = jnp.exp(jax.random.uniform(jax.random.fold_in(own, dim), (shards_of,), jnp.float32, smallest / len(cuts), top_value / len(cuts)))
        level = level * jnp.repeat(steps, dims[dim] // shards_of).reshape([-1 if axis == dim else 1 for axis in range(len(dims))])
    return level


def deal_out(key, own, number, rows, number_of, top, most, slope):
    ranking = jax.random.permutation(key, number_of)
    heavy_load, usual = shares(number_of, rows * top, most, slope, True), shares(number_of, rows * top, most, slope, False)
    places = jnp.arange(number_of)

    def named(lengths, rotation):
        used = int((lengths > 0).sum())
        fixed = max(1, used // 4)
        shifted = fixed + (places - fixed + rotation * (used - fixed)) % max(1, number_of - fixed)
        return jnp.zeros((number_of,), jnp.int32).at[ranking[jnp.where(places < fixed, places, shifted)]].set(jnp.asarray(lengths, jnp.int32))

    lengths = jnp.where(number % 4 == 0, named(heavy_load, number // 4), named(usual, number - number // 4 - 1))
    mixed = jax.random.permutation(jax.random.fold_in(own, 3), number_of)
    donor, receiver = mixed[0:number_of // 2 * 2:2], mixed[1:number_of // 2 * 2:2]
    margin = jnp.minimum(lengths[donor] - 1, most - lengths[receiver]) // 2
    margin = jnp.where((donor == ranking[0]) | (receiver == ranking[0]) | (lengths[receiver] == 0), 0, jnp.maximum(margin, 0))
    shifted = jax.random.randint(jax.random.fold_in(own, 4), (number_of // 2,), 0, 1 << 20) % (margin + 1)
    lengths = lengths.at[donor].add(-shifted).at[receiver].add(shifted)
    members = jnp.searchsorted(jnp.cumsum(lengths), jnp.arange(rows * top), side="right").astype(jnp.int32)
    grid = members.reshape(top, rows).T
    grid = grid[jax.random.permutation(jax.random.fold_in(own, 1), rows)]
    rotation = jax.random.randint(jax.random.fold_in(own, 2), (rows, 1), 0, top)
    return jnp.take_along_axis(grid, (jnp.arange(top)[None, :] + rotation) % top, axis=1)


def shares(count, total, most, slope, full):
    loads = [(1 << 20) // math.isqrt(standing ** slope) + 1 for standing in range(1, count + 1)]
    largest = most if full else min(most, max(-(-total // count), total * loads[0] // sum(loads)))
    least = 1 if total - largest >= count - 1 else 0
    given, spare = [largest] + [least] * (count - 1), total - largest - least * (count - 1)
    while spare > 0:
        movable = [i for i in range(1, count) if given[i] < largest] or [i for i in range(1, count) if given[i] < most]
        mass, remaining = sum([loads[i] for i in movable]), spare
        for i in movable:
            addition = min(most - given[i], max(1, remaining * loads[i] // mass), spare)
            given[i] = given[i] + addition
            spare = spare - addition
    return np.array(given)


def noise(own_key, shape, deviation, bound, shards=(), kind=jnp.bfloat16):
    gain = block_levels(own_key, shape, shards, -0.22, 0.18) if shards else 1.0
    entries = jax.random.normal(own_key, shape, jnp.float32) * deviation * gain
    return jnp.minimum(jnp.maximum(entries, -bound), bound).astype(kind)


def setup_inputs(seed: int = 0) -> dict:
    key_list = jax.random.split(jax.random.key(seed), 12)
    cand_tokens = noise(key_list[0], (CANDS, D), 1.0, 6.0, ((0, 128),))
    cand_user = touch_ends(jax.random.randint(key_list[1], (CANDS,), 0, USR_GRP), jax.random.fold_in(key_list[1], 1), 0, USR_GRP - 1).astype(jnp.int32)
    hist_len = touch_ends(jax.random.randint(key_list[2], (USERS,), 1, HLEN + 1), jax.random.fold_in(key_list[2], 1), 1, HLEN).astype(jnp.int32)
    req_owner_keys = jax.random.split(jax.random.fold_in(key_list[3], 1), N_GRP * N_HIST * REQ // REQ)
    req_owner_turns = jax.random.permutation(jax.random.fold_in(key_list[3], 3), N_GRP * N_HIST * REQ // REQ)
    req_owner = jax.vmap(lambda own, number: deal_out(jax.random.fold_in(key_list[3], 2), own, number, REQ, N_GRP, 1, CAP, 2))(req_owner_keys, req_owner_turns).reshape((N_GRP, N_HIST, REQ, 1))
    req_slot = touch_ends(jax.random.randint(key_list[4], (N_GRP, N_HIST, REQ), 0, OWN_DEV), jax.random.fold_in(key_list[4], 1), 0, OWN_DEV - 1).astype(jnp.int32)
    hist_embed = noise(key_list[5], (N_GRP * OWN_DEV, N_HIST, BLK, D), 1.0, 6.0, ((0, 16), (1, 8)))
    w_query = noise(key_list[6], (D, D), D ** -0.5, 0.1875)
    w_key = noise(key_list[7], (D, D), D ** -0.5, 0.1875)
    w_value = noise(key_list[8], (D, D), D ** -0.5, 0.1875)
    w_gate = noise(key_list[9], (D, D), D ** -0.5, 0.1875)
    w_out = noise(key_list[10], (D, D), D ** -0.5, 0.1875)
    return {"cand_tokens": cand_tokens, "cand_user": cand_user, "hist_len": hist_len, "req_owner": req_owner, "req_slot": req_slot, "hist_embed": hist_embed, "w_query": w_query, "w_key": w_key, "w_value": w_value, "w_gate": w_gate, "w_out": w_out}


NORM_EPS = 1e-06
LAYER_EPS = 1e-05

def rms_rows(block_rows):
    widened = block_rows.astype(jnp.float32)
    return widened * lax.rsqrt(lax.optimization_barrier(jnp.mean(widened * widened, axis=-1, keepdims=True)) + NORM_EPS)

def project(normed_rows, weight):
    return jax.nn.silu(jnp.dot(normed_rows, weight, preferred_element_type=jnp.float32))

def attend(queries, row_users, key_rows, values, key_user, key_valid):
    row_count = queries.shape[0]
    block_size = math.gcd(row_count, 512)
    scale = 1.0 / math.sqrt(HD)
    keys_heads = key_rows.astype(jnp.float32).reshape(-1, HEADS, HD)
    values_heads = values.astype(jnp.float32).reshape(-1, HEADS, HD)

    def one_block(block_index):
        first_row = block_index * block_size
        query_rows = lax.dynamic_slice_in_dim(queries, first_row, block_size, 0)
        query_rows = query_rows.astype(jnp.float32).reshape(block_size, HEADS, HD)
        users_here = lax.dynamic_slice_in_dim(row_users, first_row, block_size, 0)
        allowed = (users_here[:, None] == key_user[None, :]) & key_valid[None, :]
        scores = jnp.einsum('qhd,khd->hqk', query_rows, keys_heads) * scale
        weights = jnp.where(allowed[None], jax.nn.silu(scores), 0.0).astype(jnp.bfloat16)
        result = jnp.einsum('hqk,khd->qhd', weights.astype(jnp.float32), values_heads)
        return result.reshape(block_size, HEADS * HD)
    blocks = lax.map(one_block, jnp.arange(row_count // block_size, dtype=jnp.int32))
    return blocks.reshape(row_count, HEADS * HD)

def reference(cand_tokens, cand_user, hist_len, req_owner, req_slot, hist_embed, w_query, w_key, w_value, w_gate, w_out):
    normed_tokens = rms_rows(cand_tokens).astype(jnp.bfloat16)
    queries = project(normed_tokens, w_query).astype(jnp.bfloat16)
    gate_act = project(normed_tokens, w_gate)
    request_order = jnp.arange(REQ, dtype=jnp.int32)
    action_order = jnp.arange(BLK, dtype=jnp.int32)
    key_user = jnp.repeat(request_order // BPS, BLK).astype(jnp.int32)

    def per_group(group_id):
        group_queries = lax.dynamic_slice_in_dim(queries, group_id * CAND_GRP, CAND_GRP, 0)
        group_users = lax.dynamic_slice_in_dim(cand_user, group_id * CAND_GRP, CAND_GRP, 0)
        group_lengths = lax.dynamic_slice_in_dim(hist_len, group_id * USR_GRP, USR_GRP, 0)
        key_length = jnp.take(group_lengths, key_user, axis=0)

        def per_shard(running, shard_id):
            own_cache = lax.dynamic_index_in_dim(hist_embed, shard_id, 1, keepdims=False)
            owners = req_owner[group_id, shard_id, :, 0].astype(jnp.int32)
            slots = req_slot[group_id, shard_id].astype(jnp.int32)
            block_rows = jnp.take(own_cache, owners * OWN_DEV + slots, axis=0)
            hist_normed = rms_rows(block_rows).astype(jnp.bfloat16).reshape(REQ * BLK, D)
            key_rows = project(hist_normed, w_key).astype(jnp.bfloat16)
            values = project(hist_normed, w_value).astype(jnp.bfloat16)
            positions = ((shard_id * BPS + request_order % BPS) * BLK)[:, None] + action_order[None, :]
            key_valid = positions.reshape(-1) < key_length
            partial_value = attend(group_queries, group_users, key_rows, values, key_user, key_valid)
            return (running + partial_value, None)
        attn, _ = lax.scan(per_shard, jnp.zeros((CAND_GRP, D), jnp.float32), jnp.arange(N_HIST, dtype=jnp.int32))
        return attn
    attn = lax.map(per_group, jnp.arange(N_GRP, dtype=jnp.int32)).reshape(CANDS, D)
    centred = attn - lax.optimization_barrier(jnp.mean(attn, axis=-1, keepdims=True))
    attn_normed = centred * lax.rsqrt(lax.optimization_barrier(jnp.mean(centred * centred, axis=-1, keepdims=True)) + LAYER_EPS)
    gated = (attn_normed * gate_act).astype(jnp.bfloat16)
    mixed = cand_tokens.astype(jnp.float32) + jnp.dot(gated, w_out, preferred_element_type=jnp.float32)
    return mixed.astype(jnp.bfloat16)
```

```python
import functools
import math

import jax
import jax.numpy as jnp
from jax import lax
from jax.experimental import pallas as pl
from jax.experimental.pallas import tpu as pltpu
from jax.sharding import PartitionSpec as P

HEADS = 8
BPS = 8
NORM_EPS = 1e-06
LAYER_EPS = 1e-05
MESH = pl.DeviceIdType.MESH
F32 = jnp.float32
BF16 = jnp.bfloat16


def rms_rows(block_rows):
    widened = block_rows.astype(F32)
    return widened * lax.rsqrt(jnp.mean(widened * widened, axis=-1, keepdims=True) + NORM_EPS)


def silu(v):
    half = 0.5 * v
    return half + half * jnp.tanh(half)


def attend_kernel(group, first, meta, raw, q_ref, usr_ref, wk_ref, wv_ref, *rest):
    if first:
        out_ref, keys, values, xbuf, total, sem = rest
    else:
        acc_ref, out_ref, keys, values, xbuf, total, sem = rest
    rows, width = q_ref.shape
    blk = raw.shape[1]
    span = group * blk
    head = width // HEADS
    tile = 512
    scale = 0.5 / math.sqrt(head)

    if first:
        total[...] = jnp.zeros_like(total)
    else:
        total[...] = acc_ref[...].astype(F32)

    def fetch(user, chunk, slot):
        return [
            pltpu.make_async_copy(
                raw.at[meta[2 + user * BPS + chunk * group + i]],
                xbuf.at[slot, pl.ds(i * blk, blk)],
                sem.at[slot, i],
            )
            for i in range(group)
        ]

    for user in range(2):
        chunks = (meta[user] + group - 1) // group

        @pl.when(chunks > 0)
        def _():
            for c in fetch(user, 0, 0):
                c.start()

        @pl.loop(0, chunks)
        def _(chunk):
            slot = lax.rem(chunk, 2)

            @pl.when(chunk + 1 < chunks)
            def _():
                for c in fetch(user, chunk + 1, 1 - slot):
                    c.start()

            for c in fetch(user, chunk, slot):
                c.wait()
            normed = rms_rows(xbuf[slot]).astype(BF16)
            base = pl.multiple_of(user * BPS * blk + chunk * span, span)
            keys[pl.ds(base, span), :] = silu(
                jnp.dot(normed, wk_ref[...], preferred_element_type=F32)
            ).astype(BF16)
            projected = silu(jnp.dot(normed, wv_ref[...], preferred_element_type=F32))
            within = lax.broadcasted_iota(jnp.int32, (blk, 1), 0)
            for i in range(group):
                ok = within < meta[2 + 2 * BPS + user * BPS + chunk * group + i]
                values[pl.ds(base + i * blk, blk), :] = jnp.where(
                    ok, projected[i * blk : (i + 1) * blk], 0.0
                ).astype(BF16)

        @pl.loop(0, rows // tile)
        def _(t):
            at = pl.ds(pl.multiple_of(t * tile, tile), tile)
            mine = usr_ref[at, :] == user

            @pl.loop(0, chunks)
            def _(chunk):
                base = pl.multiple_of(user * BPS * blk + chunk * span, span)
                for h in range(HEADS):
                    cols = slice(h * head, (h + 1) * head)
                    qh = jnp.where(mine, q_ref[at, cols], jnp.zeros((), BF16))
                    scores = lax.dot_general(
                        qh,
                        keys[pl.ds(base, span), cols],
                        (((1,), (1,)), ((), ())),
                        preferred_element_type=F32,
                    )
                    half = (scores * scale).astype(BF16)
                    weights = half + half * jnp.tanh(half)
                    total[at, cols] += jnp.dot(
                        weights, values[pl.ds(base, span), cols], preferred_element_type=F32
                    )

    out_ref[...] = total[...].astype(BF16)


def attend(meta, raw, queries, users, w_key, w_value, partial, group):
    rows, width = queries.shape
    blk = raw.shape[1]
    first = partial is None
    vmem = pl.BlockSpec(memory_space=pltpu.VMEM)
    args = (meta, raw, queries, users, w_key, w_value) + (() if first else (partial,))
    specs = [pl.BlockSpec(memory_space=pltpu.SMEM), pl.BlockSpec(memory_space=pl.ANY)]
    specs += [vmem] * (len(args) - 2)
    cost = 6e9 * 4 if first else 4e9
    return pl.pallas_call(
        functools.partial(attend_kernel, group, first),
        out_shape=jax.ShapeDtypeStruct((rows, width), BF16),
        in_specs=specs,
        out_specs=vmem,
        scratch_shapes=[
            pltpu.VMEM((2 * BPS * blk, width), BF16),
            pltpu.VMEM((2 * BPS * blk, width), BF16),
            pltpu.VMEM((2, group * blk, width), BF16),
            pltpu.VMEM((rows, width), F32),
            pltpu.SemaphoreType.DMA((2, group)),
        ],
        compiler_params=pltpu.CompilerParams(vmem_limit_bytes=56 * 2**20),
        cost_estimate=pl.CostEstimate(
            flops=int(cost), bytes_accessed=20 * 2**20, transcendentals=2**24
        ),
    )(*args)


def finish_kernel(
    part, tok_ref, normed_ref, wg_ref, wo_ref, out_ref,
    mine, give, got, folded, relay, landed, lsem, csend, crecv, zsend, zrecv,
):
    grp = lax.axis_index("grp")
    shard = lax.axis_index("hist")
    z, core = shard // 2, lax.rem(shard, 2)
    up, down, far = lax.rem(z + 1, 4), lax.rem(z + 3, 4), lax.rem(z + 2, 4)
    rows = tok_ref.shape[0]
    half = rows // 2

    def device(zz, cc):
        return (grp, zz * 2 + cc)

    barrier = pltpu.get_barrier_semaphore()
    for zz, cc in ((z, 1 - core), (up, core), (down, core)):
        pl.semaphore_signal(barrier, inc=1, device_id=device(zz, cc), device_id_type=MESH)

    order = (far, up, down, z)
    loads = []
    for i, zz in enumerate(order):
        theirs = pltpu.make_async_copy(
            part.at[pl.ds((zz * 2 + 1 - core) * rows, rows)], give.at[i], lsem.at[i]
        )
        theirs.start()
        own = pltpu.make_async_copy(
            part.at[pl.ds((zz * 2 + core) * rows, rows)], mine.at[i], lsem.at[4 + i]
        )
        own.start()
        loads.append((theirs, own))
    pl.semaphore_wait(barrier, 3)

    swaps = []
    for i in range(4):
        loads[i][0].wait()
        c = pltpu.make_async_remote_copy(
            src_ref=give.at[i],
            dst_ref=got.at[i],
            send_sem=csend.at[i],
            recv_sem=crecv.at[i],
            device_id=device(z, 1 - core),
            device_id_type=MESH,
        )
        c.start()
        swaps.append(c)

    def send(src, dst, k, zz):
        c = pltpu.make_async_remote_copy(
            src_ref=src,
            dst_ref=dst,
            send_sem=zsend.at[k],
            recv_sem=zrecv.at[k],
            device_id=device(zz, core),
            device_id_type=MESH,
        )
        c.start()
        return c

    def fold(i):
        loads[i][1].wait()
        swaps[i].wait_recv()
        folded[i] = (mine[i].astype(F32) + got[i].astype(F32)).astype(BF16)

    lo, hi = slice(0, half), slice(half, rows)
    fold(0)
    s0 = send(folded.at[0, lo], relay.at[0], 0, up)
    s1 = send(folded.at[0, hi], relay.at[1], 1, down)
    fold(1)
    s2 = send(folded.at[1, hi], landed.at[0, hi], 2, up)
    fold(2)
    s3 = send(folded.at[2, lo], landed.at[1, lo], 3, down)
    gate = silu(jnp.dot(normed_ref[...], wg_ref[...], preferred_element_type=F32))
    s0.wait_recv()
    folded[1, lo] = (folded[1, lo].astype(F32) + relay[0].astype(F32)).astype(BF16)
    s4 = send(folded.at[1, lo], landed.at[0, lo], 4, up)
    s1.wait_recv()
    folded[2, hi] = (folded[2, hi].astype(F32) + relay[1].astype(F32)).astype(BF16)
    s5 = send(folded.at[2, hi], landed.at[1, hi], 5, down)
    loads[3][1].wait()
    swaps[3].wait_recv()
    own = mine[3].astype(F32) + got[3].astype(F32)
    for s in (s2, s3, s4, s5):
        s.wait_recv()
    attn = own + landed[0].astype(F32) + landed[1].astype(F32)
    centred = attn - jnp.mean(attn, axis=-1, keepdims=True)
    normed = centred * lax.rsqrt(jnp.mean(centred * centred, axis=-1, keepdims=True) + LAYER_EPS)
    gated = (normed * gate).astype(BF16)
    mixed = tok_ref[...].astype(F32) + jnp.dot(gated, wo_ref[...], preferred_element_type=F32)
    out_ref[...] = mixed.astype(BF16)
    for s in (s0, s1, s2, s3, s4, s5):
        s.wait_send()
    for s in swaps:
        s.wait_send()


def finish(partial, tokens, normed, w_gate, w_out):
    rows, width = tokens.shape
    vmem = pl.BlockSpec(memory_space=pltpu.VMEM)
    piece = pltpu.VMEM((4, rows, width), BF16)
    return pl.pallas_call(
        finish_kernel,
        out_shape=jax.ShapeDtypeStruct((rows, width), BF16),
        in_specs=[pl.BlockSpec(memory_space=pl.ANY)] + [vmem] * 4,
        out_specs=vmem,
        scratch_shapes=[
            piece,
            piece,
            piece,
            pltpu.VMEM((3, rows, width), BF16),
            pltpu.VMEM((2, rows // 2, width), BF16),
            pltpu.VMEM((2, rows, width), BF16),
            pltpu.SemaphoreType.DMA((8,)),
            pltpu.SemaphoreType.DMA((4,)),
            pltpu.SemaphoreType.DMA((4,)),
            pltpu.SemaphoreType.DMA((6,)),
            pltpu.SemaphoreType.DMA((6,)),
        ],
        compiler_params=pltpu.CompilerParams(
            collective_id=1, has_side_effects=True, vmem_limit_bytes=48 * 2**20
        ),
        cost_estimate=pl.CostEstimate(
            flops=2 * rows * width * width * 2, bytes_accessed=12 * 2**20, transcendentals=2**18
        ),
    )(partial, tokens, normed, w_gate, w_out)


def per_device(
    cand_tokens,
    cand_user,
    hist_len,
    req_owner,
    req_slot,
    hist_embed,
    w_query,
    w_key,
    w_value,
    w_gate,
    w_out,
):
    n_grp = lax.axis_size("grp")
    shard_id = lax.axis_index("hist")
    owners = req_owner[0, 0, :, 0]
    slots = req_slot[0, 0]
    req_count = owners.shape[0]
    own_cache = hist_embed[:, 0]
    blk = own_cache.shape[1]

    order = jnp.arange(req_count, dtype=jnp.int32)
    before = (owners[None, :] == owners[:, None]) & (order[None, :] < order[:, None])
    rank = jnp.sum(before.astype(jnp.int32), axis=1)
    places = jnp.arange(n_grp * 2, dtype=jnp.int32)
    chosen = places[:, None] == (owners * 2 + rank)[None, :]
    send_slots = jnp.sum(jnp.where(chosen, slots[None, :], 0), axis=1).reshape(n_grp, 2)
    asked = lax.all_to_all(send_slots, "grp", split_axis=0, concat_axis=0, tiled=True)

    user = order // BPS
    start = (shard_id * BPS + order % BPS) * blk
    valid = jnp.clip(jnp.take(hist_len, user, axis=0) - start, 0, blk)

    def listing(wave):
        counts, idx, lens = [], [], []
        for u in range(2):
            use = (rank == wave) & (valid > 0) & (user == u)
            pos = jnp.cumsum(use.astype(jnp.int32)) - 1
            hit = use[None, :] & (pos[None, :] == jnp.arange(BPS, dtype=jnp.int32)[:, None])
            counts.append(jnp.sum(use.astype(jnp.int32))[None])
            idx.append(jnp.sum(jnp.where(hit, owners[None, :], 0), axis=1))
            lens.append(jnp.sum(jnp.where(hit, valid[None, :], 0), axis=1))
        return jnp.concatenate(counts + idx + lens)

    normed_tokens = rms_rows(cand_tokens).astype(BF16)
    queries = jax.nn.silu(jnp.dot(normed_tokens, w_query, preferred_element_type=F32)).astype(BF16)
    group_queries = lax.all_gather(queries, "hist", axis=0, tiled=True)
    users = cand_user[:, None]

    partial = None
    for wave in range(2):
        sent = jnp.take(own_cache, asked[:, wave], axis=0)
        raw = lax.all_to_all(sent, "grp", split_axis=0, concat_axis=0, tiled=True)
        partial = attend(
            listing(wave), raw, group_queries, users, w_key, w_value, partial, (4, 2)[wave]
        )
    return finish(partial, cand_tokens, normed_tokens, w_gate, w_out)


def solution(mesh):
    placed = (
        P(("grp", "hist"), None),
        P("grp"),
        P("grp"),
        P("grp", "hist", None, None),
        P("grp", "hist", None),
        P("grp", "hist", None, None),
        P(),
        P(),
        P(),
        P(),
        P(),
    )
    return jax.shard_map(
        per_device, mesh=mesh, in_specs=placed, out_specs=P(("grp", "hist"), None), check_vma=False
    )
```

```python
import math

import jax
import jax.numpy as jnp
from jax import lax
from jax.experimental import pallas as pl
from jax.experimental.pallas import tpu as pltpu
from jax.sharding import PartitionSpec as P

HEADS = 8
BPS = 8
SIDE = 4
NORM_EPS = 1e-06
LAYER_EPS = 1e-05
MESH = pl.DeviceIdType.MESH
F32 = jnp.float32
BF16 = jnp.bfloat16

NEAR = ((1, 0), (3, 0), (0, 1), (0, 3))
DIAG = ((1, 1), (3, 3), (1, 3), (3, 1))
LONG = ((2, 1), (1, 2), (2, 3), (3, 2))
OPPOSITE = ((2, 2),)
STRAIGHT = ((2, 0), (0, 2))
OFFSETS = ((0, 0),) + NEAR + DIAG + LONG + OPPOSITE + STRAIGHT
SETS = (((1, 9), (9, 16)), ((1, 9), (9, 13), (13, 14), (14, 16)))
PIECES = 4
PRE = 4


def rms_rows(block_rows):
    widened = block_rows.astype(F32)
    return widened * lax.rsqrt(jnp.mean(widened * widened, axis=-1, keepdims=True) + NORM_EPS)


def silu(v):
    half = 0.5 * v
    return half + half * jnp.tanh(half)


def layer_kernel(
    tab, late, tok_ref, usr_ref, cache_hbm, wq_hbm, wk_hbm, wv_hbm, wg_hbm, wo_hbm, out_ref,
    cache, wq, wk, wv, ask_out, ask_in, asked, stage, recv, landed, q_all, umask, keys, vals, total,
    mine, give, got, folded, relay, final,
    wsem, asend, arecv, ssem, rsem, qsend, qrecv, csend, crecv, zsend, zrecv,
):
    grp = lax.axis_index("grp")
    shard = lax.axis_index("hist")
    gx, gy = grp // SIDE, lax.rem(grp, SIDE)
    z, core = shard // 2, lax.rem(shard, 2)
    up, down, far = lax.rem(z + 1, SIDE), lax.rem(z + 3, SIDE), lax.rem(z + 2, SIDE)
    rows, width = tok_ref.shape
    blk = cache.shape[1]
    head = width // HEADS
    slots = len(OFFSETS)
    half = rows // 2

    def across(dx, dy):
        return (lax.rem(gx + dx, SIDE) * SIDE + lax.rem(gy + dy, SIDE), shard)

    def back(p):
        return across((SIDE - OFFSETS[p][0]) % SIDE, (SIDE - OFFSETS[p][1]) % SIDE)

    def along(zz, cc):
        return (grp, zz * 2 + cc)

    def remote(src, dst, send_sem, recv_sem, device):
        return pltpu.make_async_remote_copy(
            src_ref=src, dst_ref=dst, send_sem=send_sem, recv_sem=recv_sem, device_id=device, device_id_type=MESH
        )

    loads = []
    for i, (src, dst) in enumerate(
        ((cache_hbm, cache), (wq_hbm, wq), (wk_hbm, wk), (wv_hbm, wv))
    ):
        c = pltpu.make_async_copy(src, dst, wsem.at[i])
        c.start()
        loads.append(c)

    barrier = pltpu.get_barrier_semaphore()
    partners = [across(*o) for o in OFFSETS[1:]] + [along(z, 1 - core), along(up, core), along(down, core)]
    for device in partners:
        pl.semaphore_signal(barrier, inc=1, device_id=device, device_id_type=MESH)
    pl.semaphore_wait(barrier, len(partners))

    lane = lax.broadcasted_iota(jnp.int32, (1, 128), 1)
    for p in range(slots):
        ask_out[p] = jnp.where(lane == 0, tab[p, 0], jnp.where(lane == 1, tab[p, 3], 0))
    asks = []
    for p in range(1, slots):
        c = remote(ask_out.at[p], ask_in.at[p], asend.at[p], arecv.at[p], back(p))
        c.start()
        asks.append(c)
    ask_in[0] = ask_out[0]

    def q_rows(zz, cc, first=0, count=None):
        return q_all.at[pl.ds(pl.multiple_of((zz * 2 + cc) * rows + first, half), count or rows)]

    def hop(k, src, device):
        c = remote(src, src, qsend.at[k], qrecv.at[k], device)
        c.start()
        return c

    normed_tokens = rms_rows(tok_ref[...]).astype(BF16)
    loads[1].wait()
    q_all[pl.ds(pl.multiple_of(shard * rows, rows), rows), :] = silu(
        jnp.dot(normed_tokens, wq[...], preferred_element_type=F32)
    ).astype(BF16)
    to_up = hop(0, q_rows(z, core), along(up, core))
    to_down = hop(1, q_rows(z, core), along(down, core))
    to_side = hop(2, q_rows(z, core), along(z, 1 - core))

    for c in asks:
        c.wait_recv()
    c = pltpu.make_async_copy(ask_in, asked, wsem.at[6])
    c.start()
    c.wait()
    loads[0].wait()
    recv[0] = cache[asked[0, 0, 0]]
    landed[0] = cache[asked[0, 0, 1]]
    step = blk // PIECES
    for wave in range(2):
        for first, last in SETS[wave]:
            for p in range(first, last):
                stage[wave * slots + p] = cache[asked[p, 0, wave]]
            for piece in range(PIECES):
                part = pl.ds(piece * step, step)
                for p in range(first, last):
                    s = wave * slots + p
                    remote(
                        stage.at[s, part], recv.at[s, part], ssem.at[s], rsem.at[s], across(*OFFSETS[p])
                    ).start()

    blocks = width // blk
    for i, src in enumerate((wg_hbm, wo_hbm)):
        c = pltpu.make_async_copy(src, cache.at[pl.ds(i * blocks, blocks)], wsem.at[4 + i])
        c.start()
        loads.append(c)

    def late_weight(i):
        loads[4 + i].wait()
        return cache[pl.ds(i * blocks, blocks)].reshape(width, width)

    def whole(s):
        return remote(stage.at[s], recv.at[s], ssem.at[s], rsem.at[s], along(z, 1 - core))

    for i in range(usr_ref.shape[0]):
        line = jnp.broadcast_to(usr_ref[i : i + 1, :].astype(F32), (128, 128))
        umask[pl.ds(i * 128, 128), :] = line.T

    to_up.wait_recv()
    on_up = hop(3, q_rows(down, core, 0, half), along(up, core))
    side_down = hop(4, q_rows(down, core), along(z, 1 - core))
    to_down.wait_recv()
    on_down = hop(5, q_rows(up, core, half, half), along(down, core))
    side_up = hop(6, q_rows(up, core), along(z, 1 - core))

    def project(x, k, n0, n1):
        normed = rms_rows(x).astype(BF16)
        keys[k] = silu(jnp.dot(normed, wk[...], preferred_element_type=F32)).astype(BF16)
        projected = silu(jnp.dot(normed, wv[...], preferred_element_type=F32)).astype(BF16)
        within = lax.broadcasted_iota(jnp.int32, (blk, 1), 0)
        zero = jnp.zeros((), BF16)
        for i in range(2):
            here = slice(i * blk, (i + 1) * blk)
            left = jnp.where(within < n0[i], projected[here], zero)
            right = jnp.where(within < n1[i], projected[here], zero)
            for h in range(HEADS):
                cols = slice(h * head, (h + 1) * head)
                vals[k, here, 2 * h * head : (2 * h + 1) * head] = left[:, cols]
                vals[k, here, (2 * h + 1) * head : (2 * h + 2) * head] = right[:, cols]

    tile = 2 * rows
    scale = 0.5 / math.sqrt(head)

    def attend_tile(zz, k, fresh=False):
        at = pl.ds(pl.multiple_of(zz * tile, tile), tile)
        first_user = umask[at, :] == 0.0
        for h in range(HEADS):
            cols = slice(h * head, (h + 1) * head)
            scores = lax.dot_general(
                q_all[at, cols], keys[k, :, cols], (((1,), (1,)), ((), ())), preferred_element_type=F32
            )
            part = (scores * scale).astype(BF16)
            weights = part + part * jnp.tanh(part)
            both = jnp.dot(
                weights, vals[k, :, 2 * h * head : (2 * h + 2) * head], preferred_element_type=F32
            )
            total[at, cols] += jnp.where(first_user, both[:, :head], both[:, head:])

    def pair(buffer, base):
        return buffer[pl.ds(base, 2)].reshape(2 * blk, width)

    def arrive(s):
        whole(s).wait_recv()

    def wave0_keys(k, buffer):
        arrive(2 * k + 1)
        project(
            pair(recv, 2 * k), buffer,
            (tab[2 * k, 1], tab[2 * k + 1, 1]), (tab[2 * k, 2], tab[2 * k + 1, 2]),
        )

    loads[2].wait()
    loads[3].wait()
    wave0_keys(0, 0)

    @pl.loop(1, PRE)
    def _(k):
        arrive(2 * k)
        wave0_keys(k, k)

    total[...] = jnp.zeros_like(total)
    on_up.wait_recv()
    on_down.wait_recv()
    side_far = hop(7, q_rows(far, core), along(z, 1 - core))
    for c in (to_side, side_down, side_up, side_far):
        c.wait_recv()

    @pl.loop(0, PRE)
    def _(k):
        @pl.loop(0, SIDE)
        def _(zz):
            attend_tile(zz, k)

    @pl.loop(PRE, slots // 2)
    def _(k):
        arrive(2 * k)
        wave0_keys(k, 0)

        @pl.loop(0, SIDE)
        def _(zz):
            attend_tile(zz, 0)

    def land(p):
        arrive(slots + p)
        landed[p] = recv[slots + p]

    def wave1_keys(k):
        a, b = 2 * k, 2 * k + 1
        x = jnp.concatenate([landed[late[a, 0]], landed[late[b, 0]]], axis=0)
        project(x, 0, (late[a, 1], late[b, 1]), (late[a, 2], late[b, 2]))

    @pl.loop(1, slots // 2)
    def _(p):
        land(p)

    @pl.loop(0, slots // 4 - 1)
    def _(k):
        land(slots // 2 + 2 * k)
        land(slots // 2 + 2 * k + 1)
        wave1_keys(k)

        @pl.loop(0, SIDE)
        def _(zz):
            attend_tile(zz, 0)

    land(slots - 2)
    land(slots - 1)
    wave1_keys(slots // 4 - 1)

    swaps = []
    for i, zz in enumerate((far, up, down, z)):
        attend_tile(zz, 0)
        for cc, dst in ((1 - core, give), (core, mine)):
            at = pl.ds(pl.multiple_of((zz * 2 + cc) * rows, rows), rows)
            sums = total[at, :]
            dst[i] = (sums - jnp.mean(sums, axis=-1, keepdims=True)).astype(BF16)
        c = remote(give.at[i], got.at[i], csend.at[i], crecv.at[i], along(z, 1 - core))
        c.start()
        swaps.append(c)

    def send(k, src, dst, zz):
        c = remote(src, dst, zsend.at[k], zrecv.at[k], along(zz, core))
        c.start()
        return c

    def fold(i):
        swaps[i].wait_recv()
        folded[i] = (mine[i].astype(F32) + got[i].astype(F32)).astype(BF16)

    lo, hi = pl.ds(0, half), pl.ds(half, half)
    fold(0)
    s0 = send(0, folded.at[0, lo], relay.at[0], up)
    s1 = send(1, folded.at[0, hi], relay.at[1], down)
    fold(1)
    s2 = send(2, folded.at[1, hi], final.at[0, hi], up)
    fold(2)
    s3 = send(3, folded.at[2, lo], final.at[1, lo], down)
    gate = silu(jnp.dot(normed_tokens, late_weight(0), preferred_element_type=F32))
    s0.wait_recv()
    folded[1, lo] = (folded[1, lo].astype(F32) + relay[0].astype(F32)).astype(BF16)
    s4 = send(4, folded.at[1, lo], final.at[0, lo], up)
    s1.wait_recv()
    folded[2, hi] = (folded[2, hi].astype(F32) + relay[1].astype(F32)).astype(BF16)
    s5 = send(5, folded.at[2, hi], final.at[1, hi], down)
    swaps[3].wait_recv()
    own = mine[3].astype(F32) + got[3].astype(F32)
    for s in (s2, s3, s4, s5):
        s.wait_recv()
    attn = own + final[0].astype(F32) + final[1].astype(F32)
    centred = attn - jnp.mean(attn, axis=-1, keepdims=True)
    normed = centred * lax.rsqrt(jnp.mean(centred * centred, axis=-1, keepdims=True) + LAYER_EPS)
    gated = (normed * gate).astype(BF16)
    mixed = tok_ref[...].astype(F32) + jnp.dot(gated, late_weight(1), preferred_element_type=F32)
    out_ref[...] = mixed.astype(BF16)

    for c in asks + [to_up, to_down, to_side, on_up, side_down, on_down, side_up, side_far] + swaps:
        c.wait_send()
    for c in (s0, s1, s2, s3, s4, s5):
        c.wait_send()
    for wave in range(2):

        @pl.loop(1, slots)
        def _(p):
            whole(wave * slots + p).wait_send()


def per_device(
    cand_tokens,
    cand_user,
    hist_len,
    req_owner,
    req_slot,
    hist_embed,
    w_query,
    w_key,
    w_value,
    w_gate,
    w_out,
):
    rows, width = cand_tokens.shape
    grp = lax.axis_index("grp")
    shard_id = lax.axis_index("hist")
    owners = req_owner[0, 0, :, 0]
    slots = req_slot[0, 0]
    req_count = owners.shape[0]
    own_cache = hist_embed[:, 0]
    blk = own_cache.shape[1]
    positions = len(OFFSETS)

    order = jnp.arange(req_count, dtype=jnp.int32)
    before = (owners[None, :] == owners[:, None]) & (order[None, :] < order[:, None])
    rank = jnp.sum(before.astype(jnp.int32), axis=1)
    user = order // BPS
    start = (shard_id * BPS + order % BPS) * blk
    valid = jnp.clip(jnp.where(user == 0, hist_len[0], hist_len[1]) - start, 0, blk)
    facts = jnp.stack([slots, jnp.where(user == 0, valid, 0), jnp.where(user == 1, valid, 0)])
    dx = jnp.array([o[0] for o in OFFSETS], jnp.int32)
    dy = jnp.array([o[1] for o in OFFSETS], jnp.int32)
    owner_at = (grp // SIDE - dx + SIDE) % SIDE * SIDE + (grp % SIDE - dy + SIDE) % SIDE
    chosen = (owners[None, None, :] == owner_at[:, None, None]) & (
        rank[None, None, :] == jnp.arange(2, dtype=jnp.int32)[None, :, None]
    )
    tab = jnp.sum(jnp.where(chosen[:, :, None, :], facts[None, None], 0), axis=-1)
    real = tab[:, 1, 1] + tab[:, 1, 2] > 0
    place = jnp.arange(positions, dtype=jnp.int32)
    behind = jnp.sum((real[None, :] & (place[None, :] > place[:, None])).astype(jnp.int32), axis=1)
    entry = jnp.arange(positions // 2, dtype=jnp.int32)
    hit = real[None, :] & (positions // 2 - 1 - behind[None, :] == entry[:, None])
    found = jnp.stack([place, tab[:, 1, 1], tab[:, 1, 2]])
    late = jnp.sum(jnp.where(hit[:, None, :], found[None], 0), axis=-1)

    smem = pl.BlockSpec(memory_space=pltpu.SMEM)
    vmem = pl.BlockSpec(memory_space=pltpu.VMEM)
    hbm = pl.BlockSpec(memory_space=pl.ANY)
    group = cand_user.shape[0]
    weight = pltpu.VMEM((width, width), BF16)
    piece = pltpu.VMEM((SIDE, rows, width), BF16)
    dma = pltpu.SemaphoreType.DMA
    return pl.pallas_call(
        layer_kernel,
        out_shape=jax.ShapeDtypeStruct((rows, width), BF16),
        in_specs=[smem, smem, vmem, vmem] + [hbm] * 6,
        out_specs=vmem,
        scratch_shapes=[
            pltpu.VMEM(own_cache.shape, BF16),
            weight, weight, weight,
            pltpu.VMEM((positions, 1, 128), jnp.int32),
            pltpu.VMEM((positions, 1, 128), jnp.int32),
            pltpu.SMEM((positions, 1, 128), jnp.int32),
            pltpu.VMEM((2 * positions, blk, width), BF16),
            pltpu.VMEM((2 * positions, blk, width), BF16),
            pltpu.VMEM((positions, blk, width), BF16),
            pltpu.VMEM((group, width), BF16),
            pltpu.VMEM((group, 128), F32),
            pltpu.VMEM((PRE, 2 * blk, width), BF16),
            pltpu.VMEM((PRE, 2 * blk, 2 * width), BF16),
            pltpu.VMEM((group, width), F32),
            piece, piece, piece,
            pltpu.VMEM((3, rows, width), BF16),
            pltpu.VMEM((2, rows // 2, width), BF16),
            pltpu.VMEM((2, rows, width), BF16),
            dma((7,)),
            dma((positions,)), dma((positions,)),
            dma((2 * positions,)), dma((2 * positions,)),
            dma((8,)), dma((8,)),
            dma((4,)), dma((4,)),
            dma((6,)), dma((6,)),
        ],
        compiler_params=pltpu.CompilerParams(
            collective_id=1, has_side_effects=True, vmem_limit_bytes=63 * 2**20
        ),
        cost_estimate=pl.CostEstimate(
            flops=int(4e10), bytes_accessed=32 * 2**20, transcendentals=2**24
        ),
    )(
        tab.reshape(positions, 6), late, cand_tokens, cand_user.reshape(group // 128, 128), own_cache,
        w_query, w_key, w_value, w_gate.reshape(-1, blk, width), w_out.reshape(-1, blk, width),
    )


def solution(mesh):
    placed = (
        P(("grp", "hist"), None),
        P("grp"),
        P("grp"),
        P("grp", "hist", None, None),
        P("grp", "hist", None),
        P("grp", "hist", None, None),
        P(),
        P(),
        P(),
        P(),
        P(),
    )
    return jax.shard_map(
        per_device, mesh=mesh, in_specs=placed, out_specs=P(("grp", "hist"), None), check_vma=False
    )
```

```python
import math

import jax
import jax.numpy as jnp
from jax import lax
from jax.experimental import pallas as pl
from jax.experimental.pallas import tpu as pltpu
from jax.sharding import PartitionSpec as P

HEADS = 8
BPS = 8
SIDE = 4
NORM_EPS = 1e-06
LAYER_EPS = 1e-05
MESH = pl.DeviceIdType.MESH
F32 = jnp.float32
BF16 = jnp.bfloat16

OFFSETS = (
    ((0, 0),)
    + ((1, 0), (3, 0), (0, 1), (0, 3))
    + ((1, 1), (3, 3), (1, 3), (3, 1))
    + ((2, 1), (2, 3), (0, 2))
    + ((1, 2), (3, 2), (2, 0))
    + ((2, 2),)
)
SETS = ((1, 9), (9, 12), (12, 15), (15, 16))
PIECES = 4
PRE = 4
DUE = (0, 2, 4, 5)
TILE = 2048


def rms_rows(block_rows):
    widened = block_rows.astype(F32)
    return widened * lax.rsqrt(jnp.mean(widened * widened, axis=-1, keepdims=True) + NORM_EPS)


def silu(v):
    half = 0.5 * v
    return half + half * jnp.tanh(half)


def layer_kernel(
    owners, wanted, lengths, tok_ref, usr_ref, cache_hbm, wq_hbm, wk_hbm, wv_hbm, wg_hbm, wo_hbm, out_ref,
    cache, wq, wk, wv, ask_out, ask_in, asked, stage, recv, landed, q_all, umask, keys, vals, total,
    mine, give, got, folded, relay, final, tab, late,
    wsem, asend, arecv, ssem, rsem, qsend, qrecv, csend, crecv, zsend, zrecv,
):
    grp = lax.axis_index("grp")
    shard = lax.axis_index("hist")
    gx, gy = grp // SIDE, lax.rem(grp, SIDE)
    z, core = shard // 2, lax.rem(shard, 2)
    up, down, far = lax.rem(z + 1, SIDE), lax.rem(z + 3, SIDE), lax.rem(z + 2, SIDE)
    rows, width = tok_ref.shape
    blk = cache.shape[1]
    head = width // HEADS
    slots = len(OFFSETS)
    half = rows // 2

    def across(dx, dy):
        return (lax.rem(gx + dx, SIDE) * SIDE + lax.rem(gy + dy, SIDE), shard)

    def back(p):
        return across((SIDE - OFFSETS[p][0]) % SIDE, (SIDE - OFFSETS[p][1]) % SIDE)

    def along(zz, cc):
        return (grp, zz * 2 + cc)

    def remote(src, dst, send_sem, recv_sem, device):
        return pltpu.make_async_remote_copy(
            src_ref=src, dst_ref=dst, send_sem=send_sem, recv_sem=recv_sem, device_id=device, device_id_type=MESH
        )

    loads = []
    for i, (src, dst) in enumerate(
        ((wq_hbm, wq), (cache_hbm, cache), (wk_hbm, wk), (wv_hbm, wv))
    ):
        c = pltpu.make_async_copy(src, dst, wsem.at[i])
        c.start()
        loads.append(c)

    barrier = pltpu.get_barrier_semaphore()
    partners = [across(*o) for o in OFFSETS[1:]] + [along(z, 1 - core), along(up, core), along(down, core)]
    for device in partners:
        pl.semaphore_signal(barrier, inc=1, device_id=device, device_id_type=MESH)
    pl.semaphore_wait(barrier, len(partners))

    count = owners.shape[0]
    named = [owners[r] for r in range(count)]
    keyed, coded = [], []
    for r in range(count):
        again = sum(((named[e] == named[r]).astype(jnp.int32) for e in range(r)), jnp.int32(0))
        keyed.append(named[r] * 2 + again)
        left = lengths[r // BPS] - (shard * BPS + r % BPS) * blk
        coded.append(wanted[r] + 16 * jnp.minimum(jnp.maximum(left, 0), blk))
    lane = lax.broadcasted_iota(jnp.int32, (1, 128), 1)
    for p in range(slots):
        owner = back(p)[0]
        asking = []
        for wave in range(2):
            found = [jnp.where(keyed[r] == owner * 2 + wave, coded[r], 0) for r in range(count)]
            one, two = sum(found[1:BPS], found[0]), sum(found[BPS + 1 :], found[BPS])
            asking.append(one % 16 + two % 16)
            tab[p, 3 * wave + 1] = one // 16
            tab[p, 3 * wave + 2] = two // 16
        ask_out[p] = jnp.where(lane == 0, asking[0], jnp.where(lane == 1, asking[1], 0))
    asks = []
    for p in range(1, slots):
        c = remote(ask_out.at[p], ask_in.at[p], asend.at[p], arecv.at[p], back(p))
        c.start()
        asks.append(c)
    ask_in[0] = ask_out[0]

    def q_rows(zz, cc, first=0, count=None):
        return q_all.at[pl.ds(pl.multiple_of((zz * 2 + cc) * rows + first, half), count or rows)]

    def hop(k, src, device):
        c = remote(src, src, qsend.at[k], qrecv.at[k], device)
        c.start()
        return c

    normed_tokens = rms_rows(tok_ref[...]).astype(BF16)
    loads[0].wait()
    q_all[pl.ds(pl.multiple_of(shard * rows, rows), rows), :] = silu(
        jnp.dot(normed_tokens, wq[...], preferred_element_type=F32)
    ).astype(BF16)
    to_up = hop(0, q_rows(z, core, 0, half), along(up, core))
    to_down = hop(1, q_rows(z, core, half, half), along(down, core))
    to_up2 = hop(8, q_rows(z, core, half, half), along(up, core))
    to_down2 = hop(9, q_rows(z, core, 0, half), along(down, core))
    to_side = hop(2, q_rows(z, core), along(z, 1 - core))

    for c in asks:
        c.wait_recv()
    c = pltpu.make_async_copy(ask_in, asked, wsem.at[6])
    c.start()
    c.wait()
    loads[1].wait()
    recv[0] = cache[asked[0, 0, 0]]
    landed[0] = cache[asked[0, 0, 1]]
    step = blk // PIECES

    def gather(wave, first, last):
        for p in range(first, last):
            stage[wave * slots + p] = cache[asked[p, 0, wave]]

    def issue(wave, part):
        first, last = SETS[part]
        for piece in range(PIECES):
            at = pl.ds(piece * step, step)
            for p in range(first, last):
                s = wave * slots + p
                remote(stage.at[s, at], recv.at[s, at], ssem.at[s], rsem.at[s], across(*OFFSETS[p])).start()

    for part in range(len(SETS)):
        gather(0, *SETS[part])
        issue(0, part)
    gather(1, 1, slots)
    blocks = width // blk
    for i, src in enumerate((wg_hbm, wo_hbm)):
        c = pltpu.make_async_copy(src, cache.at[pl.ds(i * blocks, blocks)], wsem.at[4 + i])
        c.start()
        loads.append(c)

    def late_weight(i):
        loads[4 + i].wait()
        return cache[pl.ds(i * blocks, blocks)].reshape(width, width)

    def whole(s):
        return remote(stage.at[s], recv.at[s], ssem.at[s], rsem.at[s], along(z, 1 - core))

    entry, places, codes = jnp.int32(slots // 2 - 1), [], []
    for p in reversed(range(slots)):
        n0, n1 = tab[p, 4], tab[p, 5]
        real = n0 + n1 > 0
        places.append(jnp.where(real, entry, -1))
        codes.append(p + 16 * n0 + 4096 * n1)
        entry = entry - real.astype(jnp.int32)
    for e in range(slots // 2):
        found = [jnp.where(places[i] == e, codes[i], 0) for i in range(slots)]
        code = sum(found[1:], found[0])
        late[e, 0] = code % 16
        late[e, 1] = code // 16 % 256
        late[e, 2] = code // 4096

    for i in range(usr_ref.shape[0]):
        line = jnp.broadcast_to(usr_ref[i : i + 1, :].astype(F32), (128, 128))
        umask[pl.ds(i * 128, 128), :] = line.T

    to_up.wait_recv()
    on_up = hop(3, q_rows(down, core, 0, half), along(up, core))
    to_down.wait_recv()
    on_down = hop(5, q_rows(up, core, half, half), along(down, core))
    to_up2.wait_recv()
    side_down = hop(4, q_rows(down, core), along(z, 1 - core))
    to_down2.wait_recv()
    side_up = hop(6, q_rows(up, core), along(z, 1 - core))

    def project(x, k, n0, n1):
        normed = rms_rows(x).astype(BF16)
        keys[k] = silu(jnp.dot(normed, wk[...], preferred_element_type=F32)).astype(BF16)
        projected = silu(jnp.dot(normed, wv[...], preferred_element_type=F32)).astype(BF16)
        within = lax.broadcasted_iota(jnp.int32, (blk, 1), 0)
        zero = jnp.zeros((), BF16)
        for i in range(2):
            here = slice(i * blk, (i + 1) * blk)
            left = jnp.where(within < n0[i], projected[here], zero)
            right = jnp.where(within < n1[i], projected[here], zero)
            for h in range(HEADS):
                cols = slice(h * head, (h + 1) * head)
                vals[k, here, 2 * h * head : (2 * h + 1) * head] = left[:, cols]
                vals[k, here, (2 * h + 1) * head : (2 * h + 2) * head] = right[:, cols]

    tile = 2 * rows
    scale = 0.5 / math.sqrt(head)

    def attend_rows(at, k):
        first_user = umask[at, :] == 0.0
        for h in range(HEADS):
            cols = slice(h * head, (h + 1) * head)
            scores = lax.dot_general(
                q_all[at, cols], keys[k, :, cols], (((1,), (1,)), ((), ())), preferred_element_type=F32
            )
            part = (scores * scale).astype(BF16)
            weights = part + part * jnp.tanh(part)
            both = jnp.dot(
                weights, vals[k, :, 2 * h * head : (2 * h + 2) * head], preferred_element_type=F32
            )
            total[at, cols] += jnp.where(first_user, both[:, :head], both[:, head:])

    def attend(k):
        @pl.loop(0, total.shape[0] // TILE)
        def _(t):
            attend_rows(pl.ds(pl.multiple_of(t * TILE, TILE), TILE), k)

    def pair(buffer, base):
        return buffer[pl.ds(base, 2)].reshape(2 * blk, width)

    def arrive(s):
        whole(s).wait_recv()

    def wave0_keys(k, buffer):
        arrive(2 * k + 1)
        project(
            pair(recv, 2 * k), buffer,
            (tab[2 * k, 1], tab[2 * k + 1, 1]), (tab[2 * k, 2], tab[2 * k + 1, 2]),
        )

    loads[2].wait()
    loads[3].wait()
    wave0_keys(0, 0)

    @pl.loop(1, PRE)
    def _(k):
        arrive(2 * k)
        wave0_keys(k, k)

    total[...] = jnp.zeros_like(total)
    on_up.wait_recv()
    on_down.wait_recv()
    side_far = hop(7, q_rows(far, core), along(z, 1 - core))
    for c in (to_side, side_down, side_up, side_far):
        c.wait_recv()

    def send_due(k):
        for part, due in enumerate(DUE):

            @pl.when(k == due)
            def _():
                issue(1, part)

    @pl.loop(0, PRE)
    def _(k):
        send_due(k)
        attend(k)

    @pl.loop(PRE, slots // 2)
    def _(k):
        arrive(2 * k)
        wave0_keys(k, 0)
        send_due(k)
        attend(0)

    def land(p):
        arrive(slots + p)
        landed[p] = recv[slots + p]

    def wave1_keys(k):
        a, b = 2 * k, 2 * k + 1
        x = jnp.concatenate([landed[late[a, 0]], landed[late[b, 0]]], axis=0)
        project(x, 0, (late[a, 1], late[b, 1]), (late[a, 2], late[b, 2]))

    @pl.loop(1, slots // 2)
    def _(p):
        land(p)

    @pl.loop(0, slots // 4 - 1)
    def _(k):
        land(slots // 2 + 2 * k)
        land(slots // 2 + 2 * k + 1)
        wave1_keys(k)

        attend(0)

    land(slots - 2)
    land(slots - 1)
    wave1_keys(slots // 4 - 1)

    swaps = []
    for i, zz in enumerate((far, up, down, z)):
        attend_rows(pl.ds(pl.multiple_of(zz * tile, tile), tile), 0)
        for cc, dst in ((1 - core, give), (core, mine)):
            at = pl.ds(pl.multiple_of((zz * 2 + cc) * rows, rows), rows)
            sums = total[at, :]
            dst[i] = (sums - jnp.mean(sums, axis=-1, keepdims=True)).astype(BF16)
        c = remote(give.at[i], got.at[i], csend.at[i], crecv.at[i], along(z, 1 - core))
        c.start()
        swaps.append(c)

    def send(k, src, dst, zz):
        c = remote(src, dst, zsend.at[k], zrecv.at[k], along(zz, core))
        c.start()
        return c

    def fold(i):
        swaps[i].wait_recv()
        folded[i] = (mine[i].astype(F32) + got[i].astype(F32)).astype(BF16)

    lo, hi = pl.ds(0, half), pl.ds(half, half)
    fold(0)
    s0 = send(0, folded.at[0, lo], relay.at[0], up)
    s1 = send(1, folded.at[0, hi], relay.at[1], down)
    fold(1)
    s2 = send(2, folded.at[1, hi], final.at[0, hi], up)
    fold(2)
    s3 = send(3, folded.at[2, lo], final.at[1, lo], down)
    gate = silu(jnp.dot(normed_tokens, late_weight(0), preferred_element_type=F32))
    s0.wait_recv()
    folded[1, lo] = (folded[1, lo].astype(F32) + relay[0].astype(F32)).astype(BF16)
    s4 = send(4, folded.at[1, lo], final.at[0, lo], up)
    s1.wait_recv()
    folded[2, hi] = (folded[2, hi].astype(F32) + relay[1].astype(F32)).astype(BF16)
    s5 = send(5, folded.at[2, hi], final.at[1, hi], down)
    swaps[3].wait_recv()
    own = mine[3].astype(F32) + got[3].astype(F32)
    for s in (s2, s3, s4, s5):
        s.wait_recv()
    attn = own + final[0].astype(F32) + final[1].astype(F32)
    centred = attn - jnp.mean(attn, axis=-1, keepdims=True)
    normed = centred * lax.rsqrt(jnp.mean(centred * centred, axis=-1, keepdims=True) + LAYER_EPS)
    gated = (normed * gate).astype(BF16)
    mixed = tok_ref[...].astype(F32) + jnp.dot(gated, late_weight(1), preferred_element_type=F32)
    out_ref[...] = mixed.astype(BF16)

    for c in asks + [to_up, to_down, to_up2, to_down2, to_side, on_up, side_down, on_down, side_up, side_far] + swaps:
        c.wait_send()
    for c in (s0, s1, s2, s3, s4, s5):
        c.wait_send()
    for wave in range(2):

        @pl.loop(1, slots)
        def _(p):
            whole(wave * slots + p).wait_send()


def per_device(
    cand_tokens,
    cand_user,
    hist_len,
    req_owner,
    req_slot,
    hist_embed,
    w_query,
    w_key,
    w_value,
    w_gate,
    w_out,
):
    rows, width = cand_tokens.shape
    own_cache = hist_embed[:, 0]
    blk = own_cache.shape[1]
    positions = len(OFFSETS)
    smem = pl.BlockSpec(memory_space=pltpu.SMEM)
    vmem = pl.BlockSpec(memory_space=pltpu.VMEM)
    hbm = pl.BlockSpec(memory_space=pl.ANY)
    group = cand_user.shape[0]
    weight = pltpu.VMEM((width, width), BF16)
    piece = pltpu.VMEM((SIDE, rows, width), BF16)
    dma = pltpu.SemaphoreType.DMA
    return pl.pallas_call(
        layer_kernel,
        out_shape=jax.ShapeDtypeStruct((rows, width), BF16),
        in_specs=[smem, smem, smem, vmem, vmem] + [hbm] * 6,
        out_specs=vmem,
        scratch_shapes=[
            pltpu.VMEM(own_cache.shape, BF16),
            weight, weight, weight,
            pltpu.VMEM((positions, 1, 128), jnp.int32),
            pltpu.VMEM((positions, 1, 128), jnp.int32),
            pltpu.SMEM((positions, 1, 128), jnp.int32),
            pltpu.VMEM((2 * positions, blk, width), BF16),
            pltpu.VMEM((2 * positions, blk, width), BF16),
            pltpu.VMEM((positions, blk, width), BF16),
            pltpu.VMEM((group, width), BF16),
            pltpu.VMEM((group, 128), F32),
            pltpu.VMEM((PRE, 2 * blk, width), BF16),
            pltpu.VMEM((PRE, 2 * blk, 2 * width), BF16),
            pltpu.VMEM((group, width), F32),
            piece, piece, piece,
            pltpu.VMEM((3, rows, width), BF16),
            pltpu.VMEM((2, rows // 2, width), BF16),
            pltpu.VMEM((2, rows, width), BF16),
            pltpu.SMEM((positions, 6), jnp.int32),
            pltpu.SMEM((positions // 2, 3), jnp.int32),
            dma((7,)),
            dma((positions,)), dma((positions,)),
            dma((2 * positions,)), dma((2 * positions,)),
            dma((10,)), dma((10,)),
            dma((4,)), dma((4,)),
            dma((6,)), dma((6,)),
        ],
        compiler_params=pltpu.CompilerParams(
            collective_id=1, has_side_effects=True, vmem_limit_bytes=63 * 2**20
        ),
        cost_estimate=pl.CostEstimate(
            flops=int(4e10), bytes_accessed=32 * 2**20, transcendentals=2**24
        ),
    )(
        req_owner.reshape(-1), req_slot.reshape(-1), hist_len, cand_tokens, cand_user.reshape(group // 128, 128), own_cache,
        w_query, w_key, w_value, w_gate.reshape(-1, blk, width), w_out.reshape(-1, blk, width),
    )


def solution(mesh):
    placed = (
        P(("grp", "hist"), None),
        P("grp"),
        P("grp"),
        P("grp", "hist", None, None),
        P("grp", "hist", None),
        P("grp", "hist", None, None),
        P(),
        P(),
        P(),
        P(),
        P(),
    )
    return jax.shard_map(
        per_device, mesh=mesh, in_specs=placed, out_specs=P(("grp", "hist"), None), check_vma=False
    )
```

```python
import math

import jax
import jax.numpy as jnp
from jax import lax
from jax.experimental import pallas as pl
from jax.experimental.pallas import tpu as pltpu
from jax.sharding import PartitionSpec as P

HEADS = 8
BPS = 8
SIDE = 4
NORM_EPS = 1e-06
LAYER_EPS = 1e-05
MESH = pl.DeviceIdType.MESH
F32 = jnp.float32
BF16 = jnp.bfloat16

OFFSETS = (
    ((0, 0),)
    + ((1, 0), (3, 0), (0, 1), (0, 3))
    + ((1, 1), (3, 3), (1, 3), (3, 1))
    + ((2, 1), (2, 3), (0, 2))
    + ((1, 2), (3, 2), (2, 0))
    + ((2, 2),)
)
SETS = ((1, 9), (9, 12), (12, 15), (15, 16))
PIECES = 4
PRE = 4
DUE = (0, 1, 3, 5)
TILE = 2048


def rms_rows(block_rows):
    widened = block_rows.astype(F32)
    return widened * lax.rsqrt(jnp.mean(widened * widened, axis=-1, keepdims=True) + NORM_EPS)


def silu(v):
    half = 0.5 * v
    return half + half * jnp.tanh(half)


def layer_kernel(
    owners, wanted, lengths, tok_ref, usr_ref, cache_hbm, wq_hbm, wk_hbm, wv_hbm, wg_hbm, wo_hbm, out_ref,
    cache, wq, wk, wv, ask_out, ask_in, asked, stage, recv, landed, q_all, umask, keys, vals, total,
    mine, give, got, folded, relay, final, tab, late,
    wsem, asend, arecv, ssem, rsem, qsend, qrecv, csend, crecv, zsend, zrecv,
):
    grp = lax.axis_index("grp")
    shard = lax.axis_index("hist")
    gx, gy = grp // SIDE, lax.rem(grp, SIDE)
    z, core = shard // 2, lax.rem(shard, 2)
    up, down, far = lax.rem(z + 1, SIDE), lax.rem(z + 3, SIDE), lax.rem(z + 2, SIDE)
    rows, width = tok_ref.shape
    blk = cache.shape[1]
    head = width // HEADS
    slots = len(OFFSETS)
    half = rows // 2

    def across(dx, dy):
        return (lax.rem(gx + dx, SIDE) * SIDE + lax.rem(gy + dy, SIDE), shard)

    def back(p):
        return across((SIDE - OFFSETS[p][0]) % SIDE, (SIDE - OFFSETS[p][1]) % SIDE)

    def along(zz, cc):
        return (grp, zz * 2 + cc)

    def remote(src, dst, send_sem, recv_sem, device):
        return pltpu.make_async_remote_copy(
            src_ref=src, dst_ref=dst, send_sem=send_sem, recv_sem=recv_sem, device_id=device, device_id_type=MESH
        )

    loads = []
    for i, (src, dst) in enumerate(
        ((wq_hbm, wq), (cache_hbm, cache), (wk_hbm, wk), (wv_hbm, wv))
    ):
        c = pltpu.make_async_copy(src, dst, wsem.at[i])
        c.start()
        loads.append(c)

    barrier = pltpu.get_barrier_semaphore()
    partners = [across(*o) for o in OFFSETS[1:]] + [along(z, 1 - core), along(up, core), along(down, core)]
    for device in partners:
        pl.semaphore_signal(barrier, inc=1, device_id=device, device_id_type=MESH)

    count = owners.shape[0]
    named = [owners[r] for r in range(count)]
    keyed, coded = [], []
    for r in range(count):
        again = sum(((named[e] == named[r]).astype(jnp.int32) for e in range(r)), jnp.int32(0))
        keyed.append(named[r] * 2 + again)
        left = lengths[r // BPS] - (shard * BPS + r % BPS) * blk
        coded.append(wanted[r] + 16 * jnp.minimum(jnp.maximum(left, 0), blk))
    lane = lax.broadcasted_iota(jnp.int32, (1, 128), 1)
    for p in range(slots):
        owner = back(p)[0]
        asking = []
        for wave in range(2):
            found = [jnp.where(keyed[r] == owner * 2 + wave, coded[r], 0) for r in range(count)]
            one, two = sum(found[1:BPS], found[0]), sum(found[BPS + 1 :], found[BPS])
            asking.append(one % 16 + two % 16)
            tab[p, 3 * wave + 1] = one // 16
            tab[p, 3 * wave + 2] = two // 16
        ask_out[p] = jnp.where(lane == 0, asking[0], jnp.where(lane == 1, asking[1], 0))
    pl.semaphore_wait(barrier, len(partners))
    asks = []
    for p in range(1, slots):
        c = remote(ask_out.at[p], ask_in.at[p], asend.at[p], arecv.at[p], back(p))
        c.start()
        asks.append(c)
    ask_in[0] = ask_out[0]

    def q_rows(zz, cc, first=0, count=None):
        return q_all.at[pl.ds(pl.multiple_of((zz * 2 + cc) * rows + first, half), count or rows)]

    def hop(k, src, device):
        c = remote(src, src, qsend.at[k], qrecv.at[k], device)
        c.start()
        return c

    normed_tokens = rms_rows(tok_ref[...]).astype(BF16)
    loads[0].wait()
    q_all[pl.ds(pl.multiple_of(shard * rows, rows), rows), :] = silu(
        jnp.dot(normed_tokens, wq[...], preferred_element_type=F32)
    ).astype(BF16)
    to_up = hop(0, q_rows(z, core, 0, half), along(up, core))
    to_down = hop(1, q_rows(z, core, half, half), along(down, core))
    to_up2 = hop(8, q_rows(z, core, half, half), along(up, core))
    to_down2 = hop(9, q_rows(z, core, 0, half), along(down, core))
    to_side = hop(2, q_rows(z, core), along(z, 1 - core))

    for c in asks:
        c.wait_recv()
    c = pltpu.make_async_copy(ask_in, asked, wsem.at[6])
    c.start()
    c.wait()
    loads[1].wait()
    recv[0] = cache[asked[0, 0, 0]]
    landed[0] = cache[asked[0, 0, 1]]
    step = blk // PIECES

    def gather(wave, first, last):
        for p in range(first, last):
            stage[wave * slots + p] = cache[asked[p, 0, wave]]

    def issue(wave, part):
        first, last = SETS[part]
        for piece in range(PIECES):
            at = pl.ds(piece * step, step)
            for p in range(first, last):
                s = wave * slots + p
                remote(stage.at[s, at], recv.at[s, at], ssem.at[s], rsem.at[s], across(*OFFSETS[p])).start()

    for part in range(len(SETS)):
        gather(0, *SETS[part])
        issue(0, part)
    gather(1, 1, slots)
    blocks = width // blk
    for i, src in enumerate((wg_hbm, wo_hbm)):
        c = pltpu.make_async_copy(src, cache.at[pl.ds(i * blocks, blocks)], wsem.at[4 + i])
        c.start()
        loads.append(c)

    def late_weight(i):
        loads[4 + i].wait()
        return cache[pl.ds(i * blocks, blocks)].reshape(width, width)

    def whole(s):
        return remote(stage.at[s], recv.at[s], ssem.at[s], rsem.at[s], along(z, 1 - core))

    entry, places, codes = jnp.int32(slots // 2 - 1), [], []
    for p in reversed(range(slots)):
        n0, n1 = tab[p, 4], tab[p, 5]
        real = n0 + n1 > 0
        places.append(jnp.where(real, entry, -1))
        codes.append(p + 16 * n0 + 4096 * n1)
        entry = entry - real.astype(jnp.int32)
    for e in range(slots // 2):
        found = [jnp.where(places[i] == e, codes[i], 0) for i in range(slots)]
        code = sum(found[1:], found[0])
        late[e, 0] = code % 16
        late[e, 1] = code // 16 % 256
        late[e, 2] = code // 4096

    for i in range(usr_ref.shape[0]):
        line = jnp.broadcast_to(usr_ref[i : i + 1, :].astype(F32), (128, 128))
        umask[pl.ds(i * 128, 128), :] = line.T

    to_up.wait_recv()
    on_up = hop(3, q_rows(down, core, 0, half), along(up, core))
    to_down.wait_recv()
    on_down = hop(5, q_rows(up, core, half, half), along(down, core))
    to_up2.wait_recv()
    side_down = hop(4, q_rows(down, core), along(z, 1 - core))
    to_down2.wait_recv()
    side_up = hop(6, q_rows(up, core), along(z, 1 - core))

    def project(x, k, n0, n1):
        normed = rms_rows(x).astype(BF16)
        keys[k] = silu(jnp.dot(normed, wk[...], preferred_element_type=F32)).astype(BF16)
        projected = silu(jnp.dot(normed, wv[...], preferred_element_type=F32)).astype(BF16)
        within = lax.broadcasted_iota(jnp.int32, (blk, 1), 0)
        zero = jnp.zeros((), BF16)
        for i in range(2):
            here = slice(i * blk, (i + 1) * blk)
            left = jnp.where(within < n0[i], projected[here], zero)
            right = jnp.where(within < n1[i], projected[here], zero)
            for h in range(HEADS):
                cols = slice(h * head, (h + 1) * head)
                vals[k, here, 2 * h * head : (2 * h + 1) * head] = left[:, cols]
                vals[k, here, (2 * h + 1) * head : (2 * h + 2) * head] = right[:, cols]

    tile = 2 * rows
    scale = 0.5 / math.sqrt(head)

    def attend_rows(at, k):
        first_user = umask[at, :] == 0.0
        for h in range(HEADS):
            cols = slice(h * head, (h + 1) * head)
            scores = lax.dot_general(
                q_all[at, cols], keys[k, :, cols], (((1,), (1,)), ((), ())), preferred_element_type=F32
            )
            part = (scores * scale).astype(BF16)
            weights = part + part * jnp.tanh(part)
            both = jnp.dot(
                weights, vals[k, :, 2 * h * head : (2 * h + 2) * head], preferred_element_type=F32
            )
            total[at, cols] += jnp.where(first_user, both[:, :head], both[:, head:])

    def attend(k):
        @pl.loop(0, total.shape[0] // TILE)
        def _(t):
            attend_rows(pl.ds(pl.multiple_of(t * TILE, TILE), TILE), k)

    def pair(buffer, base):
        return buffer[pl.ds(base, 2)].reshape(2 * blk, width)

    def arrive(s):
        whole(s).wait_recv()

    def wave0_keys(k, buffer):
        arrive(2 * k + 1)
        project(
            pair(recv, 2 * k), buffer,
            (tab[2 * k, 1], tab[2 * k + 1, 1]), (tab[2 * k, 2], tab[2 * k + 1, 2]),
        )

    loads[2].wait()
    loads[3].wait()
    wave0_keys(0, 0)

    @pl.loop(1, PRE)
    def _(k):
        arrive(2 * k)
        wave0_keys(k, k)

    total[...] = jnp.zeros_like(total)
    on_up.wait_recv()
    on_down.wait_recv()
    side_far = hop(7, q_rows(far, core), along(z, 1 - core))
    for c in (to_side, side_down, side_up, side_far):
        c.wait_recv()

    def send_due(k):
        for part, due in enumerate(DUE):

            @pl.when(k == due)
            def _():
                issue(1, part)

    @pl.loop(0, PRE)
    def _(k):
        send_due(k)
        attend(k)

    @pl.loop(PRE, slots // 2)
    def _(k):
        arrive(2 * k)
        wave0_keys(k, 0)
        send_due(k)
        attend(0)

    def land(p):
        arrive(slots + p)
        landed[p] = recv[slots + p]

    def wave1_keys(k):
        a, b = 2 * k, 2 * k + 1
        x = jnp.concatenate([landed[late[a, 0]], landed[late[b, 0]]], axis=0)
        project(x, 0, (late[a, 1], late[b, 1]), (late[a, 2], late[b, 2]))

    @pl.loop(1, slots // 2)
    def _(p):
        land(p)

    @pl.loop(0, slots // 4 - 1)
    def _(k):
        land(slots // 2 + 2 * k)
        land(slots // 2 + 2 * k + 1)
        wave1_keys(k)

        attend(0)

    land(slots - 2)
    land(slots - 1)
    wave1_keys(slots // 4 - 1)

    swaps = []
    for i, zz in enumerate((far, up, down, z)):
        attend_rows(pl.ds(pl.multiple_of(zz * tile, tile), tile), 0)
        for cc, dst in ((1 - core, give), (core, mine)):
            at = pl.ds(pl.multiple_of((zz * 2 + cc) * rows, rows), rows)
            sums = total[at, :]
            dst[i] = (sums - jnp.mean(sums, axis=-1, keepdims=True)).astype(BF16)
        c = remote(give.at[i], got.at[i], csend.at[i], crecv.at[i], along(z, 1 - core))
        c.start()
        swaps.append(c)

    def send(k, src, dst, zz):
        c = remote(src, dst, zsend.at[k], zrecv.at[k], along(zz, core))
        c.start()
        return c

    def fold(i):
        swaps[i].wait_recv()
        folded[i] = (mine[i].astype(F32) + got[i].astype(F32)).astype(BF16)

    lo, hi = pl.ds(0, half), pl.ds(half, half)
    fold(0)
    s0 = send(0, folded.at[0, lo], relay.at[0], up)
    s1 = send(1, folded.at[0, hi], relay.at[1], down)
    fold(1)
    s2 = send(2, folded.at[1, hi], final.at[0, hi], up)
    fold(2)
    s3 = send(3, folded.at[2, lo], final.at[1, lo], down)
    gate = silu(jnp.dot(normed_tokens, late_weight(0), preferred_element_type=F32))
    s0.wait_recv()
    folded[1, lo] = (folded[1, lo].astype(F32) + relay[0].astype(F32)).astype(BF16)
    s4 = send(4, folded.at[1, lo], final.at[0, lo], up)
    s1.wait_recv()
    folded[2, hi] = (folded[2, hi].astype(F32) + relay[1].astype(F32)).astype(BF16)
    s5 = send(5, folded.at[2, hi], final.at[1, hi], down)
    swaps[3].wait_recv()
    own = mine[3].astype(F32) + got[3].astype(F32)
    for s in (s2, s3, s4, s5):
        s.wait_recv()
    attn = own + final[0].astype(F32) + final[1].astype(F32)
    centred = attn - jnp.mean(attn, axis=-1, keepdims=True)
    normed = centred * lax.rsqrt(jnp.mean(centred * centred, axis=-1, keepdims=True) + LAYER_EPS)
    gated = (normed * gate).astype(BF16)
    mixed = tok_ref[...].astype(F32) + jnp.dot(gated, late_weight(1), preferred_element_type=F32)
    out_ref[...] = mixed.astype(BF16)

    for c in asks + [to_up, to_down, to_up2, to_down2, to_side, on_up, side_down, on_down, side_up, side_far] + swaps:
        c.wait_send()
    for c in (s0, s1, s2, s3, s4, s5):
        c.wait_send()
    for wave in range(2):

        @pl.loop(1, slots)
        def _(p):
            whole(wave * slots + p).wait_send()


def per_device(
    cand_tokens,
    cand_user,
    hist_len,
    req_owner,
    req_slot,
    hist_embed,
    w_query,
    w_key,
    w_value,
    w_gate,
    w_out,
):
    rows, width = cand_tokens.shape
    own_cache = hist_embed[:, 0]
    blk = own_cache.shape[1]
    positions = len(OFFSETS)
    smem = pl.BlockSpec(memory_space=pltpu.SMEM)
    vmem = pl.BlockSpec(memory_space=pltpu.VMEM)
    hbm = pl.BlockSpec(memory_space=pl.ANY)
    group = cand_user.shape[0]
    weight = pltpu.VMEM((width, width), BF16)
    piece = pltpu.VMEM((SIDE, rows, width), BF16)
    dma = pltpu.SemaphoreType.DMA
    return pl.pallas_call(
        layer_kernel,
        out_shape=jax.ShapeDtypeStruct((rows, width), BF16),
        in_specs=[smem, smem, smem, vmem, vmem] + [hbm] * 6,
        out_specs=vmem,
        scratch_shapes=[
            pltpu.VMEM(own_cache.shape, BF16),
            weight, weight, weight,
            pltpu.VMEM((positions, 1, 128), jnp.int32),
            pltpu.VMEM((positions, 1, 128), jnp.int32),
            pltpu.SMEM((positions, 1, 128), jnp.int32),
            pltpu.VMEM((2 * positions, blk, width), BF16),
            pltpu.VMEM((2 * positions, blk, width), BF16),
            pltpu.VMEM((positions, blk, width), BF16),
            pltpu.VMEM((group, width), BF16),
            pltpu.VMEM((group, 128), F32),
            pltpu.VMEM((PRE, 2 * blk, width), BF16),
            pltpu.VMEM((PRE, 2 * blk, 2 * width), BF16),
            pltpu.VMEM((group, width), F32),
            piece, piece, piece,
            pltpu.VMEM((3, rows, width), BF16),
            pltpu.VMEM((2, rows // 2, width), BF16),
            pltpu.VMEM((2, rows, width), BF16),
            pltpu.SMEM((positions, 6), jnp.int32),
            pltpu.SMEM((positions // 2, 3), jnp.int32),
            dma((7,)),
            dma((positions,)), dma((positions,)),
            dma((2 * positions,)), dma((2 * positions,)),
            dma((10,)), dma((10,)),
            dma((4,)), dma((4,)),
            dma((6,)), dma((6,)),
        ],
        compiler_params=pltpu.CompilerParams(
            collective_id=1, has_side_effects=True, vmem_limit_bytes=63 * 2**20
        ),
        cost_estimate=pl.CostEstimate(
            flops=int(4e10), bytes_accessed=32 * 2**20, transcendentals=2**24
        ),
    )(
        req_owner.reshape(-1), req_slot.reshape(-1), hist_len, cand_tokens, cand_user.reshape(group // 128, 128), own_cache,
        w_query, w_key, w_value, w_gate.reshape(-1, blk, width), w_out.reshape(-1, blk, width),
    )


def solution(mesh):
    placed = (
        P(("grp", "hist"), None),
        P("grp"),
        P("grp"),
        P("grp", "hist", None, None),
        P("grp", "hist", None),
        P("grp", "hist", None, None),
        P(),
        P(),
        P(),
        P(),
        P(),
    )
    return jax.shard_map(
        per_device, mesh=mesh, in_specs=placed, out_specs=P(("grp", "hist"), None), check_vma=False
    )
```
